32 devices in a mesh: dp: 8 (over z, x), basis: 4 (over y, core).
Axes of the slice: x: 2, y: 2, z: 4, core: 2. Of those that a mesh axis runs over, the one named last changes fastest.
Arguments:
- train_act: bfloat16 [512, 8192], P('dp', 'basis'), may hold values from -6 to 6
- train_err: bfloat16 [512, 28672], P('dp', 'basis'), may hold values from -6 to 6
- query_act: bfloat16 [128, 8192], P('dp', 'basis'), may hold values from -6 to 6
- query_err: bfloat16 [128, 28672], P('dp', 'basis'), may hold values from -6 to 6
- query_of: int32 [128], replicated, may hold values from 0 to 3, never falling along the last dimension, each value on 1 to 64 neighbouring positions
- train_doc: int32 [512], replicated, may hold values from 0 to 31, never falling along the last dimension, each value on 1 to 64 neighbouring positions
- basis_in: bfloat16 [8192, 8192], P('basis', 'dp'), may hold values from -0.0625 to 0.0625
- basis_out: bfloat16 [28672, 28672], P('dp', 'basis'), may hold values from -0.03125 to 0.03125
- eigvals: float32 [8192, 28672], P('dp', 'basis'), may hold values from 0.05 to 5
Outputs:
- token_scores: float32 [4, 512], P(None, 'dp')
- doc_scores: float32 [4, 32], replicated
The draws below stay inside these ranges and needn't reach their ends.
Inputs may be any that keep to these rules, and one draw needn't show every extreme that they name: `query_of`: queries are contiguous runs of query tokens, in increasing order; each query has at least one token. `train_doc`: documents are contiguous runs of training tokens, in increasing order; each document has at least one token.
All inputs are finite; a program needn't handle non-finite values.
Results may differ from the reference program's by a relative error of at most 0.0053.
Values may be sent and summed in bfloat16 or wider, within the bound.
A program may use at most 256 MiB of HBM per device.

```python
import math
import jax
import jax.numpy as jnp
import numpy as np
from jax import lax

DI = 8192
DO = 28672
NQ = 4
NDOC = 32
TOKENS = 512
QTOK = 128


def level_of(key, extent, pieces, low, high):
    def one(axis_at, parts):
        steps = jax.random.uniform(jax.random.fold_in(jax.random.fold_in(key, 6), axis_at), (parts,), jnp.float32, low / len(pieces), high / len(pieces))
        return jnp.repeat(jnp.exp(steps), extent[axis_at] // parts).reshape((-1,) + (1,) * (len(extent) - axis_at - 1))

    factor_of = one(*pieces[0])
    for cut in pieces[1:]:
        factor_of = factor_of * one(*cut)
    return factor_of


def length_profile(amount, total, reach, slope):
    portions = [(1 << 20) // math.isqrt(standing ** slope) + 1 for standing in range(2, amount + 1)]
    spare, holding = total - reach - (amount - 1), [1] * (amount - 1)
    while spare > 0:
        free = [i for i in range(amount - 1) if holding[i] < reach]
        whole, left = sum([portions[i] for i in free]), spare
        for i in free:
            addition = min(reach - holding[i], max(1, left * portions[i] // whole), spare)
            holding[i] = holding[i] + addition
            spare = spare - addition
    return np.array([reach] + holding)


def uneven_parts(key, number_of, total, most, lean):
    if number_of == 2:
        one = jax.random.randint(key, (), max(1, total - most), min(most, total - 1) + 1)
        return jnp.stack([one, total - one])
    sizes = jnp.asarray(length_profile(number_of, total, most, lean), jnp.int32)
    twos = (number_of - 1) // 2
    giver, sink = sizes[1:1 + 2 * twos:2], sizes[2:2 + 2 * twos:2]
    margin = jnp.minimum(giver - 1, most - sink)
    passed = jax.random.randint(jax.random.fold_in(key, 1), (twos,), 0, 1 << 20) % (margin + 1)
    sizes = sizes.at[1:1 + 2 * twos:2].set(giver - passed).at[2:2 + 2 * twos:2].set(sink + passed)
    return sizes[jax.random.permutation(jax.random.fold_in(key, 2), number_of)]


def normal_values(stream_key, extent, width, most, shards=(), kind=jnp.bfloat16):
    entries = jax.random.normal(stream_key, extent, jnp.float32) * width
    if len(shards) > 0:
        entries = level_of(stream_key, extent, shards, -0.22, 0.18) * entries
    return jnp.clip(entries, min=-most, max=most).astype(kind)


def setup_inputs(seed: int = 0) -> dict:
    streams_of = jax.random.split(jax.random.key(seed), 10)
    train_act = normal_values(streams_of[0], (TOKENS, DI), 1.0, 6.0, ((0, 8), (1, 4)))
    train_err = normal_values(streams_of[1], (TOKENS, DO), 1.0, 6.0, ((0, 8), (1, 4)))
    query_act = normal_values(streams_of[2], (QTOK, DI), 1.0, 6.0, ((0, 8), (1, 4)))
    query_err = normal_values(streams_of[3], (QTOK, DO), 1.0, 6.0, ((0, 8), (1, 4)))
    query_of = jnp.searchsorted(jnp.cumsum(uneven_parts(streams_of[4], NQ, QTOK, QTOK // 2, 1)), jnp.arange(QTOK), side="right").astype(jnp.int32)
    train_doc = jnp.searchsorted(jnp.cumsum(uneven_parts(streams_of[5], NDOC, TOKENS, TOKENS // 8, 1)), jnp.arange(TOKENS), side="right").astype(jnp.int32)
    basis_in = normal_values(streams_of[6], (DI, DI), DI ** -0.5, 0.0625, ((0, 4), (1, 8)))
    basis_out = normal_values(streams_of[7], (DO, DO), DO ** -0.5, 0.03125, ((0, 8), (1, 4)))
    eigvals = jnp.clip(jnp.exp(math.log(5.0) - 4.6051702 * jax.random.uniform(streams_of[8], (DI, DO), jnp.float32) ** level_of(streams_of[8], (DI, DO), ((0, 8), (1, 4)), -0.2, 0.2)), 0.05, 5.0)
    return {"train_act": train_act, "train_err": train_err, "query_act": query_act, "query_err": query_err, "query_of": query_of, "train_doc": train_doc, "basis_in": basis_in, "basis_out": basis_out, "eigvals": eigvals}


DAMPING = 0.1
SCORE_SCALE = 1e-5


def rotate(factor, eigbasis):
    return jnp.dot(factor, eigbasis, preferred_element_type=jnp.float32).astype(jnp.bfloat16)


def reference(train_act, train_err, query_act, query_err, query_of, train_doc, basis_in, basis_out, eigvals):
    train_ra = rotate(train_act, basis_in)
    query_ra = rotate(query_act, basis_in)
    train_re = rotate(train_err, basis_out)
    query_re = rotate(query_err, basis_out)
    train_re_wide = train_re.astype(jnp.float32)
    shifted = eigvals + DAMPING

    def per_query(query_index):
        selected = (query_of == query_index).astype(jnp.bfloat16)
        weighted = query_ra * selected[:, None]
        grads = jnp.dot(weighted.T, query_re, preferred_element_type=jnp.float32)
        precond = (grads / shifted).astype(jnp.bfloat16)
        lifted = jnp.dot(train_ra, precond, preferred_element_type=jnp.float32)
        return jnp.sum(lifted * train_re_wide, axis=1) * SCORE_SCALE

    token_scores = lax.map(per_query, jnp.arange(NQ, dtype=jnp.int32))
    doc_onehot = (train_doc[:, None] == jnp.arange(NDOC, dtype=jnp.int32)[None, :]).astype(jnp.float32)
    doc_scores = jnp.dot(token_scores, doc_onehot, precision=lax.Precision.HIGHEST)
    return token_scores, doc_scores
```

```python
import functools

import jax
import jax.numpy as jnp
from jax import lax
from jax.experimental import pallas as pl
from jax.experimental.pallas import tpu as pltpu
from jax.sharding import PartitionSpec as P

NQ = 4
NDOC = 32
DAMPING = 0.1
SCORE_SCALE = 1e-05
VMEM = 56 * 1024 * 1024


def tile_of(cols):
    return 256 if cols % 256 == 0 else 128


def rotate_kernel(tokens, x_ref, b_ref, train_ref, query_ref):
    out = jnp.dot(x_ref[...], b_ref[...], preferred_element_type=jnp.float32)
    train_ref[...] = out[:tokens].astype(train_ref.dtype)
    query_ref[...] = out[tokens:]


def rotate_chunk(rows, basis, tokens, chunk, cols):
    total, depth = rows.shape
    tile = tile_of(cols)
    steps = cols // tile
    return pl.pallas_call(
        functools.partial(rotate_kernel, tokens),
        grid=(steps,),
        in_specs=[
            pl.BlockSpec((total, depth), lambda j: (0, 0)),
            pl.BlockSpec((depth, tile), lambda j: (0, chunk * steps + j)),
        ],
        out_specs=[
            pl.BlockSpec((tokens, tile), lambda j: (0, j)),
            pl.BlockSpec((total - tokens, tile), lambda j: (0, j)),
        ],
        out_shape=[
            jax.ShapeDtypeStruct((tokens, cols), jnp.bfloat16),
            jax.ShapeDtypeStruct((total - tokens, cols), jnp.float32),
        ],
        compiler_params=pltpu.CompilerParams(vmem_limit_bytes=VMEM),
        cost_estimate=pl.CostEstimate(
            flops=2 * total * depth * cols,
            bytes_accessed=2 * depth * cols + 2 * total * depth + 2 * total * cols,
            transcendentals=0,
        ),
        name="rotate_err",
    )(rows, basis)


def score_kernel(weighted_ref, train_ra_ref, query_re_ref, train_re_ref, eig_ref, out_ref):
    @pl.when(pl.program_id(0) == 0)
    def _():
        out_ref[...] = jnp.zeros_like(out_ref)

    inverse = 1.0 / (eig_ref[...] + DAMPING)
    train_re = train_re_ref[...].astype(jnp.float32)
    for q in range(NQ):
        grads = jnp.dot(weighted_ref[q], query_re_ref[...], preferred_element_type=jnp.float32)
        precond = (grads * inverse).astype(jnp.bfloat16)
        lifted = jnp.dot(train_ra_ref[...], precond, preferred_element_type=jnp.float32)
        terms = lifted * train_re
        part = terms[:, :128]
        for k in range(128, terms.shape[1], 128):
            part += terms[:, k : k + 128]
        out_ref[q] += part


def score_chunk(weighted, train_ra, query_re, train_re, eigvals, chunk):
    tokens, depth = train_ra.shape
    qtok, cols = query_re.shape
    tile = tile_of(cols)
    steps = cols // tile
    return pl.pallas_call(
        score_kernel,
        grid=(steps,),
        in_specs=[
            pl.BlockSpec(weighted.shape, lambda j: (0, 0, 0)),
            pl.BlockSpec((tokens, depth), lambda j: (0, 0)),
            pl.BlockSpec((qtok, tile), lambda j: (0, j)),
            pl.BlockSpec((tokens, tile), lambda j: (0, j)),
            pl.BlockSpec((depth, tile), lambda j: (0, chunk * steps + j)),
        ],
        out_specs=pl.BlockSpec((NQ, tokens, 128), lambda j: (0, 0, 0)),
        out_shape=jax.ShapeDtypeStruct((NQ, tokens, 128), jnp.float32),
        compiler_params=pltpu.CompilerParams(vmem_limit_bytes=VMEM),
        cost_estimate=pl.CostEstimate(
            flops=2 * NQ * depth * cols * (tokens + 2 * qtok),
            bytes_accessed=4 * depth * cols + 2 * (tokens + qtok) * cols,
            transcendentals=0,
        ),
        name="score",
    )(weighted, train_ra, query_re, train_re, eigvals)


def err_columns(train_err, query_err, shards, splits):
    tok, qtok = train_err.shape[0], query_err.shape[0]
    cols = train_err.shape[1]
    rows = tok + qtok
    if tok % splits == 0 and qtok % splits == 0:
        sub_t, sub_q = tok // splits, qtok // splits
        sub = sub_t + sub_q
        err = jnp.concatenate(
            [train_err.reshape(splits, sub_t, cols), query_err.reshape(splits, sub_q, cols)],
            axis=1,
        )
        err = lax.all_to_all(err, "basis", split_axis=0, concat_axis=0, tiled=True)
        width = splits * cols // shards
        wide = jnp.transpose(err, (1, 0, 2)).reshape(sub, shards, width)
        wide = jnp.transpose(wide, (1, 0, 2))
        wide = lax.all_to_all(wide, "dp", split_axis=0, concat_axis=0, tiled=True)
        whole = lax.all_gather(wide, "basis", axis=0, tiled=False)
        whole = jnp.transpose(whole, (1, 0, 2, 3))
        train = whole[:, :, :sub_t].reshape(shards * tok, width)
        query = whole[:, :, sub_t:].reshape(shards * qtok, width)
    else:
        err = jnp.concatenate([train_err, query_err], axis=0)
        whole = lax.all_gather(err, "basis", axis=1, tiled=True)
        whole = lax.all_to_all(whole, "dp", split_axis=1, concat_axis=0, tiled=True)
        whole = whole.reshape(shards, rows, whole.shape[1])
        train = whole[:, :tok].reshape(shards * tok, -1)
        query = whole[:, tok:].reshape(shards * qtok, -1)
    return jnp.concatenate([train, query], axis=0)


def body(
    train_act, train_err, query_act, query_err, query_of, train_doc, basis_in, basis_out, eigvals
):
    shards = lax.axis_size("dp")
    splits = lax.axis_size("basis")
    tok_local = train_act.shape[0]
    tokens = tok_local * shards
    cols = basis_out.shape[1]
    chunks = 4 if cols % 1024 == 0 else 1
    width = cols // chunks

    err_rows = err_columns(train_err, query_err, shards, splits)

    act_rows = jnp.concatenate([train_act, query_act], axis=0)
    rows_local = act_rows.shape[0]
    act_part = jnp.dot(
        lax.all_gather(act_rows, "dp", axis=0, tiled=True),
        basis_in,
        preferred_element_type=jnp.float32,
    )
    act_piece = lax.psum_scatter(act_part, "basis", scatter_dimension=0, tiled=True).astype(
        jnp.bfloat16
    )
    act_rot = lax.all_gather(act_piece, "basis", axis=0, tiled=True)
    act_rot = act_rot.reshape(shards, rows_local, act_rot.shape[1])
    train_ra = act_rot[:, :tok_local].reshape(tokens, act_rot.shape[2])
    query_ra = act_rot[:, tok_local:].reshape(-1, act_rot.shape[2])
    member = (query_of[None, :] == jnp.arange(NQ, dtype=jnp.int32)[:, None]).astype(jnp.bfloat16)
    weighted = jnp.transpose(member[:, :, None] * query_ra[None], (0, 2, 1))

    total = None
    for c in range(chunks):
        train_part, query_part = rotate_chunk(err_rows, basis_out, tokens, c, width)
        train_piece = lax.psum_scatter(train_part, "dp", scatter_dimension=0, tiled=True)
        query_piece = lax.psum_scatter(query_part, "dp", scatter_dimension=0, tiled=True)
        train_re = lax.all_gather(train_piece, "dp", axis=0, tiled=True)
        query_re = lax.all_gather(query_piece.astype(jnp.bfloat16), "dp", axis=0, tiled=True)
        part = score_chunk(weighted, train_ra, query_re, train_re, eigvals, c)
        total = part if total is None else total + part
    partial_value = jnp.sum(total, axis=2) * SCORE_SCALE
    summed = lax.psum(partial_value, ("dp", "basis"))
    first_row = lax.axis_index("dp") * tok_local
    token_scores = lax.dynamic_slice_in_dim(summed, first_row, tok_local, 1)
    doc_onehot = (train_doc[:, None] == jnp.arange(NDOC, dtype=jnp.int32)[None, :]).astype(
        jnp.float32
    )
    doc_scores = jnp.dot(summed, doc_onehot, precision=lax.Precision.HIGHEST)
    return (token_scores, doc_scores)


def solution(mesh):
    placed = (
        P("dp", "basis"),
        P("dp", "basis"),
        P("dp", "basis"),
        P("dp", "basis"),
        P(),
        P(),
        P("basis", "dp"),
        P("dp", "basis"),
        P("dp", "basis"),
    )
    return jax.shard_map(
        body, mesh=mesh, in_specs=placed, out_specs=(P(None, "dp"), P()), check_vma=False
    )
```

```python
import functools

import jax
import jax.numpy as jnp
from jax import lax
from jax.experimental import pallas as pl
from jax.experimental.pallas import tpu as pltpu
from jax.sharding import PartitionSpec as P

NQ = 4
NDOC = 32
DAMPING = 0.1
SCORE_SCALE = 1e-05
VMEM = 56 * 1024 * 1024


def tile_of(cols):
    return 256 if cols % 256 == 0 else 128


def rotate_kernel(half, x_ref, b_ref, keep_ref, send_ref):
    out = jnp.dot(x_ref[...], b_ref[...], preferred_element_type=jnp.float32)
    keep_ref[...] = out[:half]
    send_ref[...] = out[half:].astype(send_ref.dtype)


def rotate_chunk(rows, basis, chunk, cols):
    total, depth = rows.shape
    half = total // 2
    tile = tile_of(cols)
    steps = cols // tile
    return pl.pallas_call(
        functools.partial(rotate_kernel, half),
        grid=(steps,),
        in_specs=[
            pl.BlockSpec((total, depth), lambda j: (0, 0)),
            pl.BlockSpec((depth, tile), lambda j: (0, chunk * steps + j)),
        ],
        out_specs=[
            pl.BlockSpec((half, tile), lambda j: (0, j)),
            pl.BlockSpec((half, tile), lambda j: (0, j)),
        ],
        out_shape=[
            jax.ShapeDtypeStruct((half, cols), jnp.float32),
            jax.ShapeDtypeStruct((half, cols), jnp.bfloat16),
        ],
        compiler_params=pltpu.CompilerParams(vmem_limit_bytes=VMEM),
        cost_estimate=pl.CostEstimate(
            flops=2 * total * depth * cols,
            bytes_accessed=2 * depth * cols + 2 * total * depth + 3 * total * cols,
            transcendentals=0,
        ),
        name="rotate_err",
    )(rows, basis)


def score_kernel(weighted_ref, train_ra_ref, query_re_ref, train_re_ref, eig_ref, out_ref):
    @pl.when(pl.program_id(0) == 0)
    def _():
        out_ref[...] = jnp.zeros_like(out_ref)

    inverse = 1.0 / (eig_ref[...] + DAMPING)
    train_re = train_re_ref[...].astype(jnp.float32)
    for q in range(NQ):
        grads = jnp.dot(weighted_ref[q], query_re_ref[...], preferred_element_type=jnp.float32)
        precond = (grads * inverse).astype(jnp.bfloat16)
        lifted = jnp.dot(train_ra_ref[...], precond, preferred_element_type=jnp.float32)
        terms = lifted * train_re
        part = terms[:, :128]
        for k in range(128, terms.shape[1], 128):
            part += terms[:, k : k + 128]
        out_ref[q] += part


def score_chunk(weighted, train_ra, query_re, train_re, eigvals, chunk):
    tokens, depth = train_ra.shape
    qtok, cols = query_re.shape
    tile = tile_of(cols)
    steps = cols // tile
    return pl.pallas_call(
        score_kernel,
        grid=(steps,),
        in_specs=[
            pl.BlockSpec(weighted.shape, lambda j: (0, 0, 0)),
            pl.BlockSpec((tokens, depth), lambda j: (0, 0)),
            pl.BlockSpec((qtok, tile), lambda j: (0, j)),
            pl.BlockSpec((tokens, tile), lambda j: (0, j)),
            pl.BlockSpec((depth, tile), lambda j: (0, chunk * steps + j)),
        ],
        out_specs=pl.BlockSpec((NQ, tokens, 128), lambda j: (0, 0, 0)),
        out_shape=jax.ShapeDtypeStruct((NQ, tokens, 128), jnp.float32),
        compiler_params=pltpu.CompilerParams(vmem_limit_bytes=VMEM),
        cost_estimate=pl.CostEstimate(
            flops=2 * NQ * depth * cols * (tokens + 2 * qtok),
            bytes_accessed=4 * depth * cols + 2 * (tokens + qtok) * cols,
            transcendentals=0,
        ),
        name="score",
    )(weighted, train_ra, query_re, train_re, eigvals)


def swap(value, axis, offset):
    size = lax.axis_size(axis)
    return lax.ppermute(value, axis, [(i, i ^ offset) for i in range(size)])


def err_columns(train_err, query_err, shards, splits, order):
    tok, qtok = train_err.shape[0], query_err.shape[0]
    cols = train_err.shape[1]
    rows = tok + qtok
    me_d, me_b = lax.axis_index("dp"), lax.axis_index("basis")
    if tok % splits == 0 and qtok % splits == 0 and splits & (splits - 1) == 0:
        sub_t, sub_q = tok // splits, qtok // splits
        sub = sub_t + sub_q
        err = jnp.concatenate(
            [train_err.reshape(splits, sub_t, cols), query_err.reshape(splits, sub_q, cols)],
            axis=1,
        )
        pick = lambda x, i: lax.dynamic_index_in_dim(x, i, 0, keepdims=False)
        parts = [pick(err, me_b)]
        for s in range(1, splits):
            parts.append(swap(pick(err, me_b ^ s), "basis", s))
        parts = jnp.stack(parts)
        width = splits * cols // shards
        per = cols // width
        blocks = {}
        for r in range(shards):
            target = me_d ^ r
            piece = pick(parts, me_b ^ (target // per))
            piece = lax.dynamic_slice_in_dim(piece, (target % per) * width, width, 1)
            blocks[r] = piece if r == 0 else swap(piece, "dp", r)
        whole = jnp.stack([blocks[r] for r in order])[:, None]
        inner = [0]
        step = splits // 2
        while step:
            whole = jnp.concatenate([whole, swap(whole, "basis", step)], axis=1)
            inner = inner + [i ^ step for i in inner]
            step //= 2
        train = whole[:, :, :sub_t].reshape(shards, tok, width)
        query = whole[:, :, sub_t:].reshape(shards, qtok, width)
        who = me_b ^ jnp.array(inner, jnp.int32)
        train_at = (who[:, None] * sub_t + jnp.arange(sub_t, dtype=jnp.int32)).reshape(tok)
        query_at = (who[:, None] * sub_q + jnp.arange(sub_q, dtype=jnp.int32)).reshape(qtok)
        whole = jnp.concatenate([train, query], axis=1)
    else:
        err = jnp.concatenate([train_err, query_err], axis=0)
        whole = lax.all_gather(err, "basis", axis=1, tiled=True)
        whole = lax.all_to_all(whole, "dp", split_axis=1, concat_axis=0, tiled=True)
        whole = whole.reshape(shards, rows, whole.shape[1])
        whole = jnp.stack(
            [lax.dynamic_index_in_dim(whole, me_d ^ r, 0, keepdims=False) for r in order]
        )
        train_at = jnp.arange(tok, dtype=jnp.int32)
        query_at = jnp.arange(qtok, dtype=jnp.int32)
    return whole.reshape(shards * rows, -1), train_at, query_at


def body(
    train_act, train_err, query_act, query_err, query_of, train_doc, basis_in, basis_out, eigvals
):
    shards = lax.axis_size("dp")
    splits = lax.axis_size("basis")
    half = shards // 2
    me = lax.axis_index("dp")
    order = [2 * k for k in range(half)] + [2 * k + 1 for k in range(half)]
    tok_local, qtok_local = train_act.shape[0], query_act.shape[0]
    rows_local = tok_local + qtok_local
    tokens, qtokens = tok_local * shards, qtok_local * shards
    cols = basis_out.shape[1]
    chunks = 4 if cols % 1024 == 0 else 1
    width = cols // chunks

    err_rows, train_at, query_at = err_columns(train_err, query_err, shards, splits, order)
    owner = me ^ jnp.array(order, jnp.int32)
    train_at = (owner[:, None] * tok_local + train_at).reshape(tokens)
    query_at = (owner[:, None] * qtok_local + query_at).reshape(qtokens)
    train_move = train_at[:, None] == jnp.arange(tokens, dtype=jnp.int32)
    query_move = query_at[:, None] == jnp.arange(qtokens, dtype=jnp.int32)

    act_rows = jnp.concatenate([train_act, query_act], axis=0)
    act_part = jnp.dot(
        lax.all_gather(act_rows, "dp", axis=0, tiled=True),
        basis_in,
        preferred_element_type=jnp.float32,
    )
    act_piece = lax.psum_scatter(act_part, "basis", scatter_dimension=0, tiled=True).astype(
        jnp.bfloat16
    )
    act_rot = lax.all_gather(act_piece, "basis", axis=0, tiled=True)
    act_rot = act_rot.reshape(shards, rows_local, act_rot.shape[1])
    train_ra = act_rot[:, :tok_local].reshape(tokens, act_rot.shape[2])
    query_ra = act_rot[:, tok_local:].reshape(qtokens, act_rot.shape[2])
    train_ra = jnp.dot(
        train_move.astype(jnp.bfloat16), train_ra, preferred_element_type=jnp.float32
    ).astype(jnp.bfloat16)
    query_ra = jnp.dot(
        query_move.astype(jnp.bfloat16), query_ra, preferred_element_type=jnp.float32
    ).astype(jnp.bfloat16)
    query_here = jnp.sum(jnp.where(query_move, query_of[None, :], 0), axis=1)
    member = (query_here[None, :] == jnp.arange(NQ, dtype=jnp.int32)[:, None]).astype(jnp.bfloat16)
    weighted = jnp.transpose(member[:, :, None] * query_ra[None], (0, 2, 1))

    total = None
    for c in range(chunks):
        keep, send = rotate_chunk(err_rows, basis_out, c, width)
        pair = keep + swap(send, "dp", 1).astype(jnp.float32)
        pair = pair.reshape(half, rows_local, width)
        own = pair[0]
        for k in range(1, half):
            own = own + swap(pair[k].astype(jnp.bfloat16), "dp", 2 * k).astype(jnp.float32)
        own = own.astype(jnp.bfloat16)
        held = jnp.stack([own] + [swap(own, "dp", 2 * k) for k in range(1, half)])
        held = jnp.concatenate([held, swap(held, "dp", 1)], axis=0)
        train_re = held[:, :tok_local].reshape(tokens, width)
        query_re = held[:, tok_local:].reshape(qtokens, width)
        part = score_chunk(weighted, train_ra, query_re, train_re, eigvals, c)
        total = part if total is None else total + part
    summed = jnp.sum(total, axis=2) * SCORE_SCALE
    summed = jnp.dot(summed, train_move.astype(jnp.float32), precision=lax.Precision.HIGHEST)
    for axis, size in (("basis", splits), ("dp", shards)):
        step = 1
        while step < size:
            summed = summed + swap(summed, axis, step)
            step *= 2
    token_scores = lax.dynamic_slice_in_dim(summed, me * tok_local, tok_local, 1)
    doc_onehot = (train_doc[:, None] == jnp.arange(NDOC, dtype=jnp.int32)[None, :]).astype(
        jnp.float32
    )
    doc_scores = jnp.dot(summed, doc_onehot, precision=lax.Precision.HIGHEST)
    return (token_scores, doc_scores)


def solution(mesh):
    placed = (
        P("dp", "basis"),
        P("dp", "basis"),
        P("dp", "basis"),
        P("dp", "basis"),
        P(),
        P(),
        P("basis", "dp"),
        P("dp", "basis"),
        P("dp", "basis"),
    )
    return jax.shard_map(
        body, mesh=mesh, in_specs=placed, out_specs=(P(None, "dp"), P()), check_vma=False
    )
```

```python
import functools

import jax
import jax.numpy as jnp
from jax import lax
from jax.experimental import pallas as pl
from jax.experimental.pallas import tpu as pltpu
from jax.sharding import PartitionSpec as P

NQ = 4
NDOC = 32
DAMPING = 0.1
SCORE_SCALE = 1e-05
VMEM = 56 * 1024 * 1024


def tile_of(cols):
    return 256 if cols % 256 == 0 else 128


def rotate_kernel(half, x_ref, b_ref, keep_ref, send_ref):
    out = jnp.dot(x_ref[...], b_ref[...], preferred_element_type=jnp.float32)
    keep_ref[...] = out[:half]
    send_ref[...] = out[half:].astype(send_ref.dtype)


def rotate_chunk(rows, basis, chunk, cols):
    total, depth = rows.shape
    half = total // 2
    tile = tile_of(cols)
    steps = cols // tile
    return pl.pallas_call(
        functools.partial(rotate_kernel, half),
        grid=(steps,),
        in_specs=[
            pl.BlockSpec((total, depth), lambda j: (0, 0)),
            pl.BlockSpec((depth, tile), lambda j: (0, chunk * steps + j)),
        ],
        out_specs=[
            pl.BlockSpec((half, tile), lambda j: (0, j)),
            pl.BlockSpec((half, tile), lambda j: (0, j)),
        ],
        out_shape=[
            jax.ShapeDtypeStruct((half, cols), jnp.float32),
            jax.ShapeDtypeStruct((half, cols), jnp.bfloat16),
        ],
        compiler_params=pltpu.CompilerParams(vmem_limit_bytes=VMEM),
        cost_estimate=pl.CostEstimate(
            flops=2 * total * depth * cols,
            bytes_accessed=2 * depth * cols + 2 * total * depth + 3 * total * cols,
            transcendentals=0,
        ),
        name="rotate_err",
    )(rows, basis)


def score_kernel(weighted_ref, train_ra_ref, query_re_ref, train_re_ref, eig_ref, out_ref):
    @pl.when(pl.program_id(0) == 0)
    def _():
        out_ref[...] = jnp.zeros_like(out_ref)

    inverse = 1.0 / (eig_ref[...] + DAMPING)
    train_re = train_re_ref[...].astype(jnp.float32)
    for q in range(NQ):
        grads = jnp.dot(weighted_ref[q], query_re_ref[...], preferred_element_type=jnp.float32)
        precond = (grads * inverse).astype(jnp.bfloat16)
        lifted = jnp.dot(train_ra_ref[...], precond, preferred_element_type=jnp.float32)
        terms = lifted * train_re
        part = terms[:, :128]
        for k in range(128, terms.shape[1], 128):
            part += terms[:, k : k + 128]
        out_ref[q] += part


def score_chunk(weighted, train_ra, query_re, train_re, eigvals, chunk):
    tokens, depth = train_ra.shape
    qtok, cols = query_re.shape
    tile = tile_of(cols)
    steps = cols // tile
    return pl.pallas_call(
        score_kernel,
        grid=(steps,),
        in_specs=[
            pl.BlockSpec(weighted.shape, lambda j: (0, 0, 0)),
            pl.BlockSpec((tokens, depth), lambda j: (0, 0)),
            pl.BlockSpec((qtok, tile), lambda j: (0, j)),
            pl.BlockSpec((tokens, tile), lambda j: (0, j)),
            pl.BlockSpec((depth, tile), lambda j: (0, chunk * steps + j)),
        ],
        out_specs=pl.BlockSpec((NQ, tokens, 128), lambda j: (0, 0, 0)),
        out_shape=jax.ShapeDtypeStruct((NQ, tokens, 128), jnp.float32),
        compiler_params=pltpu.CompilerParams(vmem_limit_bytes=VMEM),
        cost_estimate=pl.CostEstimate(
            flops=2 * NQ * depth * cols * (tokens + 2 * qtok),
            bytes_accessed=4 * depth * cols + 2 * (tokens + qtok) * cols,
            transcendentals=0,
        ),
        name="score",
    )(weighted, train_ra, query_re, train_re, eigvals)


def swap(value, axis, offset):
    size = lax.axis_size(axis)
    return lax.ppermute(value, axis, [(i, i ^ offset) for i in range(size)])


def err_columns(train_err, query_err, shards, splits, order):
    tok, qtok = train_err.shape[0], query_err.shape[0]
    cols = train_err.shape[1]
    rows = tok + qtok
    me_d, me_b = lax.axis_index("dp"), lax.axis_index("basis")
    if tok % splits == 0 and qtok % splits == 0 and splits & (splits - 1) == 0:
        sub_t, sub_q = tok // splits, qtok // splits
        sub = sub_t + sub_q
        err = jnp.concatenate(
            [train_err.reshape(splits, sub_t, cols), query_err.reshape(splits, sub_q, cols)],
            axis=1,
        )
        pick = lambda x, i: lax.dynamic_index_in_dim(x, i, 0, keepdims=False)
        parts = [pick(err, me_b)]
        for s in range(1, splits):
            parts.append(swap(pick(err, me_b ^ s), "basis", s))
        parts = jnp.stack(parts)
        width = splits * cols // shards
        per = cols // width
        blocks = {}
        for r in range(shards):
            target = me_d ^ r
            piece = pick(parts, me_b ^ (target // per))
            piece = lax.dynamic_slice_in_dim(piece, (target % per) * width, width, 1)
            blocks[r] = piece if r == 0 else swap(piece, "dp", r)
        whole = jnp.stack([blocks[r] for r in order])[:, None]
        inner = [0]
        step = splits // 2
        while step:
            whole = jnp.concatenate([whole, swap(whole, "basis", step)], axis=1)
            inner = inner + [i ^ step for i in inner]
            step //= 2
        train = whole[:, :, :sub_t].reshape(shards, tok, width)
        query = whole[:, :, sub_t:].reshape(shards, qtok, width)
        who = me_b ^ jnp.array(inner, jnp.int32)
        train_at = (who[:, None] * sub_t + jnp.arange(sub_t, dtype=jnp.int32)).reshape(tok)
        query_at = (who[:, None] * sub_q + jnp.arange(sub_q, dtype=jnp.int32)).reshape(qtok)
        whole = jnp.concatenate([train, query], axis=1)
    else:
        err = jnp.concatenate([train_err, query_err], axis=0)
        whole = lax.all_gather(err, "basis", axis=1, tiled=True)
        whole = lax.all_to_all(whole, "dp", split_axis=1, concat_axis=0, tiled=True)
        whole = whole.reshape(shards, rows, whole.shape[1])
        whole = jnp.stack(
            [lax.dynamic_index_in_dim(whole, me_d ^ r, 0, keepdims=False) for r in order]
        )
        train_at = jnp.arange(tok, dtype=jnp.int32)
        query_at = jnp.arange(qtok, dtype=jnp.int32)
    return whole.reshape(shards * rows, -1), train_at, query_at


def body(
    train_act, train_err, query_act, query_err, query_of, train_doc, basis_in, basis_out, eigvals
):
    shards = lax.axis_size("dp")
    splits = lax.axis_size("basis")
    half = shards // 2
    me = lax.axis_index("dp")
    order = [0]
    step = half // 2
    while step:
        order = order + [k ^ (2 * step) for k in order]
        step //= 2
    order = order + [k ^ 1 for k in order]
    tok_local, qtok_local = train_act.shape[0], query_act.shape[0]
    rows_local = tok_local + qtok_local
    tokens, qtokens = tok_local * shards, qtok_local * shards
    cols = basis_out.shape[1]
    chunks = 7 if cols % 1792 == 0 else 1
    width = cols // chunks

    err_rows, train_at, query_at = err_columns(train_err, query_err, shards, splits, order)
    owner = me ^ jnp.array(order, jnp.int32)
    train_at = (owner[:, None] * tok_local + train_at).reshape(tokens)
    query_at = (owner[:, None] * qtok_local + query_at).reshape(qtokens)
    train_move = train_at[:, None] == jnp.arange(tokens, dtype=jnp.int32)
    query_move = query_at[:, None] == jnp.arange(qtokens, dtype=jnp.int32)

    act_rows = jnp.concatenate([train_act, query_act], axis=0)
    act_part = jnp.dot(
        lax.all_gather(act_rows, "dp", axis=0, tiled=True),
        basis_in,
        preferred_element_type=jnp.float32,
    )
    act_piece = lax.psum_scatter(act_part, "basis", scatter_dimension=0, tiled=True).astype(
        jnp.bfloat16
    )
    act_rot = lax.all_gather(act_piece, "basis", axis=0, tiled=True)
    act_rot = act_rot.reshape(shards, rows_local, act_rot.shape[1])
    train_ra = act_rot[:, :tok_local].reshape(tokens, act_rot.shape[2])
    query_ra = act_rot[:, tok_local:].reshape(qtokens, act_rot.shape[2])
    train_ra = jnp.dot(
        train_move.astype(jnp.bfloat16), train_ra, preferred_element_type=jnp.float32
    ).astype(jnp.bfloat16)
    query_ra = jnp.dot(
        query_move.astype(jnp.bfloat16), query_ra, preferred_element_type=jnp.float32
    ).astype(jnp.bfloat16)
    query_here = jnp.sum(jnp.where(query_move, query_of[None, :], 0), axis=1)
    member = (query_here[None, :] == jnp.arange(NQ, dtype=jnp.int32)[:, None]).astype(jnp.bfloat16)
    weighted = jnp.transpose(member[:, :, None] * query_ra[None], (0, 2, 1))

    halvings = []
    step = 1
    while step < half:
        halvings.append(2 * step)
        step *= 2
    stages = 2 * len(halvings) + 2

    def advance(stage, state):
        if stage == 0:
            keep, send = state
            return keep + swap(send, "dp", 1).astype(jnp.float32)
        if stage <= len(halvings):
            cut = state.shape[0] // 2
            send = state[cut:].astype(jnp.bfloat16)
            return state[:cut] + swap(send, "dp", halvings[stage - 1]).astype(jnp.float32)
        held = state.astype(jnp.bfloat16)
        offset = 1 if stage == stages - 1 else halvings[stages - 2 - stage]
        return jnp.concatenate([held, swap(held, "dp", offset)], axis=0)

    total = jnp.zeros((NQ, tokens, 128), jnp.float32)
    states = {0: rotate_chunk(err_rows, basis_out, 0, width)}
    for t in range(chunks + stages):
        states, err_rows, total = lax.optimization_barrier((states, err_rows, total))
        following = {}
        for c, state in states.items():
            if t - c < stages:
                following[c] = advance(t - c, state)
            else:
                held = state.reshape(shards, rows_local, width)
                train_re = held[:, :tok_local].reshape(tokens, width)
                query_re = held[:, tok_local:].reshape(qtokens, width)
                total = total + score_chunk(weighted, train_ra, query_re, train_re, eigvals, c)
        if t + 1 < chunks:
            following[t + 1] = rotate_chunk(err_rows, basis_out, t + 1, width)
        states = following
    summed = jnp.sum(total, axis=2) * SCORE_SCALE
    summed = jnp.dot(summed, train_move.astype(jnp.float32), precision=lax.Precision.HIGHEST)
    for axis, size in (("basis", splits), ("dp", shards)):
        step = 1
        while step < size:
            summed = summed + swap(summed, axis, step)
            step *= 2
    token_scores = lax.dynamic_slice_in_dim(summed, me * tok_local, tok_local, 1)
    doc_onehot = (train_doc[:, None] == jnp.arange(NDOC, dtype=jnp.int32)[None, :]).astype(
        jnp.float32
    )
    doc_scores = jnp.dot(summed, doc_onehot, precision=lax.Precision.HIGHEST)
    return (token_scores, doc_scores)


def solution(mesh):
    placed = (
        P("dp", "basis"),
        P("dp", "basis"),
        P("dp", "basis"),
        P("dp", "basis"),
        P(),
        P(),
        P("basis", "dp"),
        P("dp", "basis"),
        P("dp", "basis"),
    )
    return jax.shard_map(
        body, mesh=mesh, in_specs=placed, out_specs=(P(None, "dp"), P()), check_vma=False
    )
```
